128 devices in a mesh: ctx: 32 (over x, y, core), tp: 4 (over z).
Axes of the slice: x: 4, y: 4, z: 4, core: 2. Of those that a mesh axis runs over, the one named last changes fastest.
Arguments:
- tokens: bfloat16 [16384, 4096], P('ctx'), may hold values from -6 to 6
- query_weight: bfloat16 [4096, 512], P(None, 'tp'), may hold values from -0.09375 to 0.09375
- key_weight: bfloat16 [4096, 512], P(None, 'tp'), may hold values from -0.09375 to 0.09375
- value_weight: bfloat16 [4096, 4096], P(None, 'tp'), may hold values from -0.09375 to 0.09375
- norm_gain: bfloat16 [4096], P('tp'), may hold values from 0.5 to 1.5
- out_weight: bfloat16 [4096, 4096], P('tp'), may hold values from -0.09375 to 0.09375
Outputs:
- attended: bfloat16 [16384, 4096], P('ctx', 'tp')
The draws below stay inside these ranges and needn't reach their ends.
All inputs are finite; a program needn't handle non-finite values.
Results may differ from the reference program's by a relative error of at most 0.03.
Values may be sent and summed in bfloat16 or wider, within the bound.
A program may use at most 128 MiB of HBM per device.

```python
import jax
import jax.numpy as jnp
from jax import lax

D = 4096
H = 32
F = 16
DV = 128
TOK_DEV = 512
TOKENS = 16384
N_CTX = 32
N_TP = 4


def block_scale(stream_key, shape, split, least, largest):
    factor_of = 1.0
    for position, blocks in split:
        draws = jax.random.uniform(jax.random.fold_in(jax.random.fold_in(stream_key, 6), position), (blocks,), jnp.float32, least / len(split), largest / len(split))
        factor_of = factor_of * jnp.repeat(jnp.exp(draws), shape[position] // blocks).reshape((-1,) + (1,) * (len(shape) - 1 - position))
    return factor_of


def normal_values(stream_key, extent, scale, limit, shards=(), kind=jnp.bfloat16):
    array = scale * jax.random.normal(stream_key, extent, jnp.float32)
    if shards:
        array = array * block_scale(stream_key, extent, shards, -0.22, 0.18)
    return jnp.clip(array, -limit, limit).astype(kind)


def setup_inputs(seed: int = 0) -> dict:
    splits = jax.random.split(jax.random.key(seed), 7)
    tokens = normal_values(splits[0], (TOKENS, D), 1.0, 6.0, ((0, 32),))
    query_weight = normal_values(splits[1], (D, H * F), D ** -0.5, 0.09375, ((1, 4),))
    key_weight = normal_values(splits[2], (D, H * F), D ** -0.5, 0.09375, ((1, 4),))
    value_weight = normal_values(splits[3], (D, H * DV), D ** -0.5, 0.09375, ((1, 4),))
    norm_gain = jnp.clip(1.0 + 0.1 * jax.random.normal(splits[4], (H * DV,), jnp.float32), 0.5, 1.5).astype(jnp.bfloat16)
    out_weight = normal_values(splits[5], (H * DV, D), (H * DV) ** -0.5, 0.09375, ((0, 4),))
    return dict(tokens=tokens, query_weight=query_weight, key_weight=key_weight, value_weight=value_weight, norm_gain=norm_gain, out_weight=out_weight)


half_root = 0.7071067811865476

def widen(values):
    return lax.optimization_barrier(values).astype(jnp.float32)

def project(inputs, weight, factor):
    return (jnp.dot(inputs, weight, preferred_element_type=jnp.float32) * factor).astype(jnp.bfloat16)

def pairs_of(features):
    rows, heads, width = features.shape
    wide = widen(features)
    outer = wide[:, :, :, None] * wide[:, :, None, :] * half_root
    return outer.reshape(rows, heads, width * width).astype(jnp.bfloat16)

def reference(tokens, query_weight, key_weight, value_weight, norm_gain, out_weight):
    highest = lax.Precision.HIGHEST
    factor = F ** (-0.25)
    out_wide = out_weight.astype(jnp.float32).reshape(N_TP, H // N_TP * DV, D)
    gain_heads = norm_gain.astype(jnp.float32).reshape(H, DV)
    causal_mask = jnp.tril(jnp.ones((TOK_DEV, TOK_DEV), jnp.float32)) > 0.5

    def shard_step(carried, inputs):
        x_shard, shard_index = inputs
        prev_pairs, prev_linear, prev_values, prev_pair_sums, prev_key_sums = carried
        query_rows = project(x_shard, query_weight, factor).reshape(TOK_DEV, H, F)
        key_rows = project(x_shard, key_weight, factor).reshape(TOK_DEV, H, F)
        value_rows = project(x_shard, value_weight, 1.0).reshape(TOK_DEV, H, DV)
        query_pairs = pairs_of(query_rows)
        key_pairs = pairs_of(key_rows)
        query_wide = widen(query_rows)
        key_wide = widen(key_rows)
        value_wide = widen(value_rows)
        qpair_wide = widen(query_pairs)
        kpair_wide = widen(key_pairs)
        local_pairs = jnp.einsum('thp,thd->hpd', kpair_wide, value_wide)
        local_linear = jnp.einsum('thf,thd->hfd', key_wide, value_wide)
        local_values = lax.optimization_barrier(jnp.sum(value_wide, axis=0))
        local_pair_sums = lax.optimization_barrier(jnp.sum(kpair_wide, axis=0))
        local_key_sums = lax.optimization_barrier(jnp.sum(key_wide, axis=0))
        scores = jnp.einsum('thf,shf->hts', query_wide, key_wide)
        local_weights = jnp.where(causal_mask[None], 1.0 + scores + 0.5 * scores * scores, 0.0)
        rounded_weights = widen(local_weights.astype(jnp.bfloat16))
        numerator = prev_values[None] + jnp.einsum('thf,hfd->thd', query_wide, prev_linear, precision=highest)
        numerator = numerator + jnp.einsum('thp,hpd->thd', qpair_wide, prev_pairs, precision=highest)
        numerator = numerator + jnp.einsum('hts,shd->thd', rounded_weights, value_wide)
        denominator = shard_index.astype(jnp.float32) * TOK_DEV + jnp.einsum('thf,hf->th', query_wide, prev_key_sums, precision=highest)
        denominator = denominator + jnp.einsum('thp,hp->th', qpair_wide, prev_pair_sums, precision=highest)
        denominator = denominator + jnp.transpose(lax.optimization_barrier(jnp.sum(local_weights, axis=2)))
        ratio = numerator / denominator[:, :, None]
        spread = lax.optimization_barrier(jnp.mean(ratio * ratio, axis=2, keepdims=True))
        normalized = (ratio / jnp.sqrt(spread + 1e-06) * gain_heads[None]).astype(jnp.bfloat16)
        grouped = widen(normalized).reshape(TOK_DEV, N_TP, H // N_TP * DV)
        partial_value = jnp.einsum('tgi,gid->gtd', grouped, out_wide).astype(jnp.bfloat16)
        attended = lax.optimization_barrier(jnp.sum(widen(partial_value), axis=0)).astype(jnp.bfloat16)
        new_carry = (prev_pairs + local_pairs, prev_linear + local_linear, prev_values + local_values, prev_pair_sums + local_pair_sums, prev_key_sums + local_key_sums)
        return (new_carry, attended)
    initial = (jnp.zeros((H, F * F, DV), jnp.float32), jnp.zeros((H, F, DV), jnp.float32), jnp.zeros((H, DV), jnp.float32), jnp.zeros((H, F * F), jnp.float32), jnp.zeros((H, F), jnp.float32))
    final_states, outputs = lax.scan(shard_step, initial, (tokens.reshape(N_CTX, TOK_DEV, D), jnp.arange(N_CTX, dtype=jnp.int32)))
    return outputs.reshape(N_CTX * TOK_DEV, D)
```

```python
import functools

import jax
import jax.numpy as jnp
from jax import lax
from jax.experimental import pallas as pl
from jax.experimental.pallas import tpu as pltpu
from jax.sharding import PartitionSpec as P

MESH = pl.DeviceIdType.MESH
F = 16
DV = 128
HEADS = 8
HALF = 4
ROWS = 512
FEATS = 160
TILE = 256
RB = 4
RR = ROWS // RB
f32 = jnp.float32
bf16 = jnp.bfloat16


def iota(shape, axis):
    return lax.broadcasted_iota(jnp.int32, shape, axis)


def dot(a, b):
    return jnp.dot(a, b, preferred_element_type=f32)


def kernel(
    x_hbm, wq_hbm, wk_hbm, wv_hbm, gain_ref, wo_hbm, out_ref,
    x, wqk, wv, wo, q32, kt32, ktb, phi, vext, pick1, pick2, qext, acc, ps,
    send0, recv0, mine, send1, recv1, send2, recv2, send3, recv3,
    norm, far_s, far_r, near_s, near_r, comb, own,
    in_sem, wv_sem, wo_sem,
    s0, r0, s1, r1, s2, r2, s3, r3, fs, fr, ns, nr,
):
    ctx = lax.axis_index("ctx")
    z = lax.axis_index("tp")
    core = lax.rem(ctx, 2)
    cy = lax.rem(lax.div(ctx, 2), 4)
    cx = lax.div(ctx, 8)

    def at(px, py, pc, pz):
        return ((px * 4 + py) * 2 + pc, pz)

    partner = at(cx, cy, 1 - core, z)

    copies = [
        pltpu.make_async_copy(x_hbm, x, in_sem.at[0]),
        pltpu.make_async_copy(wk_hbm, wqk.at[:, pl.ds(128, 128)], in_sem.at[1]),
        pltpu.make_async_copy(wq_hbm, wqk.at[:, pl.ds(0, 128)], in_sem.at[2]),
    ]
    for c in copies:
        c.start()

    def wv_copy(i):
        block = lax.rem(2 * (1 - core) + i, 4)
        return pltpu.make_async_copy(
            wv_hbm.at[:, pl.ds(pl.multiple_of(block * 256, 256), 256)], wv.at[i], wv_sem.at[i]
        )

    def wo_copy(k):
        chunk = lax.rem(z + k, 4)
        return pltpu.make_async_copy(
            wo_hbm.at[:, pl.ds(pl.multiple_of(chunk * 1024, 1024), 1024)], wo.at[k], wo_sem.at[k]
        )

    for i in range(4):
        wv_copy(i).start()
    for k in (2, 1, 3, 0):
        wo_copy(k).start()

    barrier = pltpu.get_barrier_semaphore()
    peers = [partner]
    for d in (1, 2, 3):
        peers.append(at(lax.rem(cx + d, 4), cy, core, z))
        peers.append(at(cx, lax.rem(cy + d, 4), core, z))
    for d in (1, 3):
        peers.append(at(cx, cy, core, lax.rem(z + d, 4)))
    for p in peers:
        pl.semaphore_signal(barrier, inc=1, device_id=p, device_id_type=MESH)

    row = iota((256, FEATS), 0) - 112
    col = iota((256, FEATS), 1)
    low = col % 16
    first = jnp.where(col < 136, low, col - 136)
    second = (low + col // 16) % 16
    pick1[...] = jnp.where((row == first) & (col < 152), 1.0, 0.0).astype(bf16)
    pick2[...] = jnp.where((row == second) & (col < 136), 1.0, 0.0).astype(bf16)
    phi[:, pl.ds(FEATS, 256 - FEATS), :] = jnp.zeros((HEADS, 256 - FEATS, ROWS), bf16)
    vext[:, :, pl.ds(DV, DV)] = jnp.ones((HEADS, ROWS, DV), bf16)

    for c in copies:
        c.wait()
    qk = (dot(x[...], wqk[...]) * 0.5).astype(bf16).astype(f32)
    q32[...] = qk[:, 0:128]
    kt = qk[:, 128:256].T
    kt32[...] = kt
    ktb[...] = kt.astype(bf16)

    ones16 = jnp.ones((16, ROWS), bf16)

    def key_features(h, _):
        k = kt32[pl.ds(pl.multiple_of(h * 16, 16), 16), :]
        parts = [k * k * 0.5]
        for o in range(1, 8):
            parts.append(k * pltpu.roll(k, 16 - o, 0))
        parts.append(k[0:8] * k[8:16])
        parts.append(k)
        parts.append(jnp.where(iota((8, ROWS), 0) == 0, 1.0, 0.0))
        phi[h, pl.ds(0, FEATS), :] = jnp.concatenate(parts, axis=0).astype(bf16)
        return 0

    lax.fori_loop(0, HEADS, key_features, 0)

    def values(i):
        wv_copy(i).wait()
        block = lax.rem(2 * (1 - core) + i, 4)
        v = dot(x[...], wv[i]).astype(bf16)
        vext[2 * block, :, pl.ds(0, DV)] = v[:, 0:128]
        vext[2 * block + 1, :, pl.ds(0, DV)] = v[:, 128:256]

    def state(h):
        p = phi[h, pl.ds(0, FEATS), :]
        st = dot(p, vext[h, :, pl.ds(0, DV)])
        nt = (((1,), (1,)), ((), ()))
        sums0 = lax.dot_general(ones16, phi[h, pl.ds(0, 128), :], nt, preferred_element_type=f32)
        sums1 = lax.dot_general(ones16, phi[h, pl.ds(128, 128), :], nt, preferred_element_type=f32)
        i8 = iota((8, DV), 0)
        last = st[152:160] + jnp.where(i8 == 1, sums0[0:8], 0.0) + jnp.where(i8 == 2, sums1[0:8], 0.0)
        return jnp.concatenate([st[0:152], last], axis=0)

    other_base = HALF * (1 - core)
    my_base = HALF * core

    values(0)
    values(1)

    def other_states(i, _):
        send0[i] = state(other_base + i).astype(bf16)
        return 0

    lax.fori_loop(0, HALF, other_states, 0)

    pl.semaphore_wait(barrier, len(peers))

    def remote(src, dst, ss, rs, dev):
        return pltpu.make_async_remote_copy(
            src_ref=src, dst_ref=dst, send_sem=ss, recv_sem=rs, device_id=dev, device_id_type=MESH
        )

    copy0 = remote(send0, recv0, s0, r0, partner)
    copy0.start()

    values(2)
    values(3)

    def my_states(i, _):
        mine[i] = state(my_base + i)
        return 0

    lax.fori_loop(0, HALF, my_states, 0)
    copy0.wait_recv()
    send1[...] = (mine[pl.ds(0, HALF)] + recv0[...].astype(f32)).astype(bf16)

    pa = jnp.where(core == 0, cy, cx)
    pb = jnp.where(core == 0, cx, cy)

    def on_axes(a, b):
        return at(jnp.where(core == 0, b, a), jnp.where(core == 0, a, b), core, z)

    copies1 = []
    for n, d in enumerate((2, 1, 3)):
        copies1.append(remote(send1, recv1.at[n], s1.at[n], r1.at[n], on_axes(lax.rem(pa + d, 4), pb)))
    for c in copies1:
        c.start()

    c1 = jnp.where(iota((1, FEATS), 1) == 152, 1.0, 0.0)
    c2 = jnp.where((iota((1, FEATS), 1) >= 136) & (iota((1, FEATS), 1) <= 152), 1.0, 0.0)

    def local(h, _):
        q = q32[...]
        qm = jnp.where(iota((ROWS, 128), 1) // 16 == h, q, 0.0).astype(bf16)
        at_row = pl.ds(pl.multiple_of((7 - h) * 16, 16), 128)
        qb = q.astype(bf16)
        f1 = dot(qb, pick1[at_row, :]) + c1
        f2 = dot(qb, pick2[at_row, :]) + c2
        qext[h] = (f1 * f2).astype(bf16)
        below = iota((TILE, TILE), 1) <= iota((TILE, TILE), 0)
        for tb in range(ROWS // TILE):
            span = (tb + 1) * TILE
            r = dot(qm[tb * TILE : span], ktb[:, pl.ds(0, span)])
            w = (0.5 * r + 1.0) * r + 1.0
            diag = jnp.where(below, w[:, tb * TILE : span], 0.0).astype(bf16)
            a = dot(diag, vext[h, pl.ds(tb * TILE, TILE), :])
            if tb:
                a = a + dot(w[:, 0 : tb * TILE].astype(bf16), vext[h, pl.ds(0, tb * TILE), :])
            acc[h, pl.ds(tb * TILE, TILE), :] = a
        return 0

    lax.fori_loop(0, HALF, local, 0)

    for c in copies1:
        c.wait_recv()

    is1 = jnp.where(core == 1, 1.0, 0.0).astype(f32)
    senders = [lax.rem(pa + 4 - d, 4) for d in (2, 1, 3)]
    before = [jnp.where(s < pa, 1.0, 0.0).astype(f32) for s in senders]

    def sums_first(i, _):
        got = [recv1[n, i].astype(f32) for n in range(3)]
        mid = send1[i].astype(f32)
        pre = before[0] * got[0] + before[1] * got[1] + before[2] * got[2]
        every = got[0] + got[1] + got[2]
        send2[0, i] = (is1 * pre).astype(bf16)
        send2[1, i] = (mid + is1 * pre + (1.0 - is1) * every).astype(bf16)
        base = pre
        mine[i + HALF] = base
        return 0

    lax.fori_loop(0, HALF, sums_first, 0)

    copies2 = []
    for n, d in enumerate((2, 1, 3)):
        to = lax.rem(pb + d, 4)
        kind = jnp.where(to > pb, 1, 0)
        copies2.append(remote(send2.at[kind], recv2.at[n], s2.at[n], r2.at[n], on_axes(pa, to)))
    for c in copies2:
        c.start()

    lax.fori_loop(HALF, HEADS, local, 0)

    for c in copies2:
        c.wait_recv()

    def set_prefix(h, tile):
        ps[h, :, pl.ds(0, DV)] = tile.astype(bf16)
        rounded = tile[152:160]
        row0 = jnp.broadcast_to(rounded[1:2], (DV, DV))
        row1 = jnp.broadcast_to(rounded[2:3], (DV, DV))
        ps[h, pl.ds(0, 128), pl.ds(DV, DV)] = row0.T.astype(bf16)
        ps[h, pl.ds(128, 32), pl.ds(DV, DV)] = row1.T[0:32].astype(bf16)

    def sums_second(i, _):
        chips = mine[i + HALF] + recv2[0, i].astype(f32) + recv2[1, i].astype(f32) + recv2[2, i].astype(f32)
        send3[i] = (chips + (1.0 - is1) * mine[i]).astype(bf16)
        mine[i + HALF] = chips + is1 * recv0[i].astype(f32)
        return 0

    lax.fori_loop(0, HALF, sums_second, 0)
    copy3 = remote(send3, recv3, s3, r3, partner)
    copy3.start()

    def my_prefix(i, _):
        set_prefix(my_base + i, mine[i + HALF])
        return 0

    lax.fori_loop(0, HALF, my_prefix, 0)
    copy3.wait_recv()

    def other_prefix(i, _):
        set_prefix(other_base + i, recv3[i].astype(f32))
        return 0

    lax.fori_loop(0, HALF, other_prefix, 0)

    for k in range(4):
        wo_copy(k).wait()

    up = at(cx, cy, core, lax.rem(z + 1, 4))
    down = at(cx, cy, core, lax.rem(z + 3, 4))
    ways = (up, down)

    def far_copy(w, r):
        return remote(far_s.at[w, r], far_r.at[w, r], fs.at[w, r], fr.at[w, r], ways[w])

    def near_copy(w, kind, r):
        return remote(
            near_s.at[w, kind, r], near_r.at[w, kind, r], ns.at[w, kind, r], nr.at[w, kind, r], ways[w]
        )

    def rows_phase(r, _):
        at_rows = pl.ds(pl.multiple_of(r * RR, RR), RR)
        for h in range(HEADS):
            a = acc[h, at_rows, :] + dot(qext[h, at_rows, :], ps[h])
            ratio = a[:, 0:DV] / a[:, DV : 2 * DV]
            spread = jnp.mean(ratio * ratio, axis=1, keepdims=True)
            gain = gain_ref[:, pl.ds(h * DV, DV)].astype(f32)
            norm[:, pl.ds(h * DV, DV)] = (ratio * lax.rsqrt(spread + 1e-6) * gain).astype(bf16)

        def part(k, half):
            return dot(norm[...], wo[k, :, pl.ds(half * 512, 512)])

        for w in range(2):
            far_s[w, r] = part(2, w).astype(bf16)
            far_copy(w, r).start()
        near_s[0, 0, r] = part(1, 1).astype(bf16)
        near_copy(0, 0, r).start()
        near_s[1, 0, r] = part(3, 0).astype(bf16)
        near_copy(1, 0, r).start()
        comb[0, r] = part(1, 0)
        comb[1, r] = part(3, 1)
        own[r, :, pl.ds(0, 512)] = part(0, 0)
        own[r, :, pl.ds(512, 512)] = part(0, 1)
        return 0

    lax.fori_loop(0, RB, rows_phase, 0)

    def combine(r, _):
        for w in range(2):
            far_copy(w, r).wait_recv()
            near_s[w, 1, r] = (comb[w, r] + far_r[w, r].astype(f32)).astype(bf16)
            near_copy(w, 1, r).start()
        return 0

    lax.fori_loop(0, RB, combine, 0)

    def finish(r, _):
        for w in range(2):
            for kind in range(2):
                near_copy(w, kind, r).wait_recv()
        at_rows = pl.ds(pl.multiple_of(r * RR, RR), RR)
        left = own[r, :, pl.ds(0, 512)] + near_r[0, 1, r].astype(f32) + near_r[1, 0, r].astype(f32)
        right = own[r, :, pl.ds(512, 512)] + near_r[0, 0, r].astype(f32) + near_r[1, 1, r].astype(f32)
        out_ref[at_rows, pl.ds(0, 512)] = left.astype(bf16)
        out_ref[at_rows, pl.ds(512, 512)] = right.astype(bf16)
        return 0

    lax.fori_loop(0, RB, finish, 0)

    copy0.wait_send()
    for c in copies1 + copies2:
        c.wait_send()
    copy3.wait_send()

    def sent(r, _):
        for w in range(2):
            far_copy(w, r).wait_send()
            for kind in range(2):
                near_copy(w, kind, r).wait_send()
        return 0

    lax.fori_loop(0, RB, sent, 0)


def per_device(tokens, query_weight, key_weight, value_weight, norm_gain, out_weight):
    dma = pltpu.SemaphoreType.DMA
    hbm = pl.BlockSpec(memory_space=pl.ANY)
    vmem = pl.BlockSpec(memory_space=pltpu.VMEM)
    d = tokens.shape[1]
    return pl.pallas_call(
        kernel,
        out_shape=jax.ShapeDtypeStruct((ROWS, 1024), bf16),
        in_specs=[hbm, hbm, hbm, hbm, vmem, hbm],
        out_specs=vmem,
        scratch_shapes=[
            pltpu.VMEM((ROWS, d), bf16),
            pltpu.VMEM((d, 256), bf16),
            pltpu.VMEM((4, d, 256), bf16),
            pltpu.VMEM((4, 1024, 1024), bf16),
            pltpu.VMEM((ROWS, 128), f32),
            pltpu.VMEM((128, ROWS), f32),
            pltpu.VMEM((128, ROWS), bf16),
            pltpu.VMEM((HEADS, 256, ROWS), bf16),
            pltpu.VMEM((HEADS, ROWS, 2 * DV), bf16),
            pltpu.VMEM((256, FEATS), bf16),
            pltpu.VMEM((256, FEATS), bf16),
            pltpu.VMEM((HEADS, ROWS, FEATS), bf16),
            pltpu.VMEM((HEADS, ROWS, 2 * DV), f32),
            pltpu.VMEM((HEADS, FEATS, 2 * DV), bf16),
            pltpu.VMEM((HALF, FEATS, DV), bf16),
            pltpu.VMEM((HALF, FEATS, DV), bf16),
            pltpu.VMEM((2 * HALF, FEATS, DV), f32),
            pltpu.VMEM((HALF, FEATS, DV), bf16),
            pltpu.VMEM((3, HALF, FEATS, DV), bf16),
            pltpu.VMEM((2, HALF, FEATS, DV), bf16),
            pltpu.VMEM((3, HALF, FEATS, DV), bf16),
            pltpu.VMEM((HALF, FEATS, DV), bf16),
            pltpu.VMEM((HALF, FEATS, DV), bf16),
            pltpu.VMEM((RR, 1024), bf16),
            pltpu.VMEM((2, RB, RR, 512), bf16),
            pltpu.VMEM((2, RB, RR, 512), bf16),
            pltpu.VMEM((2, 2, RB, RR, 512), bf16),
            pltpu.VMEM((2, 2, RB, RR, 512), bf16),
            pltpu.VMEM((2, RB, RR, 512), f32),
            pltpu.VMEM((RB, RR, 1024), f32),
            dma((3,)),
            dma((4,)),
            dma((4,)),
            dma, dma, dma((3,)), dma((3,)), dma((3,)), dma((3,)), dma, dma,
            dma((2, RB)), dma((2, RB)), dma((2, 2, RB)), dma((2, 2, RB)),
        ],
        compiler_params=pltpu.CompilerParams(
            collective_id=0, has_side_effects=True, vmem_limit_bytes=60 * 1024 * 1024
        ),
    )(tokens, query_weight, key_weight, value_weight, norm_gain.reshape(1, -1), out_weight)


def solution(mesh):
    in_specs = (P("ctx", None), P(None, "tp"), P(None, "tp"), P(None, "tp"), P("tp"), P("tp", None))
    out_specs = P("ctx", "tp")
    return jax.shard_map(
        per_device, mesh=mesh, in_specs=in_specs, out_specs=out_specs, check_vma=False
    )
```

```python
import functools

import jax
import jax.numpy as jnp
from jax import lax
from jax.experimental import pallas as pl
from jax.experimental.pallas import tpu as pltpu
from jax.sharding import PartitionSpec as P

MESH = pl.DeviceIdType.MESH
DV = 128
HEADS = 8
HALF = 4
ROWS = 512
FEATS = 160
TILE = 256
PAIR = 2
TURNS = (3, 6)
DISTANCES = (2, 1, 3)
SLOTS = ((2, 0), (2, 1), (1, 1), (3, 0), (1, 0), (3, 1), (0, 0), (0, 1))
RB = 4
RR = ROWS // RB
f32 = jnp.float32
bf16 = jnp.bfloat16


def iota(shape, axis):
    return lax.broadcasted_iota(jnp.int32, shape, axis)


def dot(a, b):
    return jnp.dot(a, b, preferred_element_type=f32)


def kernel(
    x_hbm, wq_hbm, wk_hbm, wv_hbm, gain_ref, wo_hbm, out_hbm,
    x, w, wo, proj, q32, kt32, ktb, phi, vext, pick1, pick2, qext, acc, ps,
    states, send0, recv0, send1, recv1, base, send2, recv2, send3, recv3,
    norm, zs, zr, part32, obuf,
    in_sem, w_sem, wo_sem, out_sem,
    s0, r0, s1, r1, s2, r2, s3, r3, zss, zrs,
):
    ctx = lax.axis_index("ctx")
    z = lax.axis_index("tp")
    core = lax.rem(ctx, 2)
    cy = lax.rem(lax.div(ctx, 2), 4)
    cx = lax.div(ctx, 8)

    def at(px, py, pc, pz):
        return ((px * 4 + py) * 2 + pc, pz)

    partner = at(cx, cy, 1 - core, z)

    x_copy = pltpu.make_async_copy(x_hbm, x, in_sem.at[0])
    k_copy = pltpu.make_async_copy(wk_hbm, w.at[0, :, pl.ds(128, 128)], in_sem.at[1])
    q_copy = pltpu.make_async_copy(wq_hbm, w.at[0, :, pl.ds(0, 128)], in_sem.at[2])
    for c in (x_copy, k_copy, q_copy):
        c.start()

    def block_of(i):
        return lax.rem(2 * (1 - core) + i - 1, 4)

    def wv_copy(i):
        columns = pl.ds(pl.multiple_of(block_of(i) * 256, 256), 256)
        return pltpu.make_async_copy(wv_hbm.at[:, columns], w.at[i], w_sem.at[i])

    for i in range(1, 5):
        wv_copy(i).start()

    def wo_copy(j):
        chunk, half = SLOTS[j]
        first = lax.rem(z + chunk, 4) * 1024 + half * 512
        columns = pl.ds(pl.multiple_of(first, 512), 512)
        return pltpu.make_async_copy(wo_hbm.at[:, columns], wo.at[j], wo_sem.at[j])

    barrier = pltpu.get_barrier_semaphore()
    peers = [partner]
    for d in (1, 2, 3):
        peers.append(at(lax.rem(cx + d, 4), cy, core, z))
        peers.append(at(cx, lax.rem(cy + d, 4), core, z))
    for d in (1, 3):
        peers.append(at(cx, cy, core, lax.rem(z + d, 4)))
    for p in peers:
        pl.semaphore_signal(barrier, inc=1, device_id=p, device_id_type=MESH)

    def remote(src, dst, ss, rs, dev):
        return pltpu.make_async_remote_copy(
            src_ref=src, dst_ref=dst, send_sem=ss, recv_sem=rs, device_id=dev, device_id_type=MESH
        )

    row = iota((256, FEATS), 0) - 112
    col = iota((256, FEATS), 1)
    low = col & 15
    first = jnp.where(col < 136, low, col - 136)
    second = (low + (col >> 4)) & 15
    pick1[...] = jnp.where((row == first) & (col < 152), 1.0, 0.0).astype(bf16)
    pick2[...] = jnp.where((row == second) & (col < 136), 1.0, 0.0).astype(bf16)
    phi[:, pl.ds(FEATS, 256 - FEATS), :] = jnp.zeros((HEADS, 256 - FEATS, ROWS), bf16)
    vext[:, :, pl.ds(DV, DV)] = jnp.ones((HEADS, ROWS, DV), bf16)

    ones16 = jnp.ones((16, ROWS), bf16)

    def key_features(h, _):
        k = kt32[pl.ds(pl.multiple_of(h * 16, 16), 16), :]
        parts = [k * k * 0.5]
        for o in range(1, 8):
            parts.append(k * pltpu.roll(k, 16 - o, 0))
        parts.append(k[0:8] * k[8:16])
        parts.append(k)
        parts.append(jnp.where(iota((8, ROWS), 0) == 0, 1.0, 0.0))
        phi[h, pl.ds(0, FEATS), :] = jnp.concatenate(parts, axis=0).astype(bf16)
        return 0

    def state(h):
        p = phi[h, pl.ds(0, FEATS), :]
        st = dot(p, vext[h, :, pl.ds(0, DV)])
        nt = (((1,), (1,)), ((), ()))
        sums0 = lax.dot_general(ones16, phi[h, pl.ds(0, 128), :], nt, preferred_element_type=f32)
        sums1 = lax.dot_general(ones16, phi[h, pl.ds(128, 128), :], nt, preferred_element_type=f32)
        i8 = iota((8, DV), 0)
        last = st[152:160] + jnp.where(i8 == 1, sums0[0:8], 0.0) + jnp.where(i8 == 2, sums1[0:8], 0.0)
        return jnp.concatenate([st[0:152], last], axis=0)

    pa = jnp.where(core == 0, cy, cx)
    pb = jnp.where(core == 0, cx, cy)

    def on_axes(a, b):
        return at(jnp.where(core == 0, b, a), jnp.where(core == 0, a, b), core, z)

    def copy0(c):
        return remote(send0.at[c], recv0.at[c], s0.at[c], r0.at[c], partner)

    def copies1(c):
        return [
            remote(send1.at[c], recv1.at[n, c], s1.at[n, c], r1.at[n, c], on_axes(lax.rem(pa + d, 4), pb))
            for n, d in enumerate(DISTANCES)
        ]

    def copies2(c):
        out = []
        for n, d in enumerate(DISTANCES):
            to = lax.rem(pb + d, 4)
            kind = jnp.where(to > pb, 1, 0)
            out.append(remote(send2.at[kind, c], recv2.at[n, c], s2.at[n, c], r2.at[n, c], on_axes(pa, to)))
        return out

    def copy3(c):
        return remote(send3.at[c], recv3.at[c], s3.at[c], r3.at[c], partner)

    def project(i, _):
        @pl.when(i == 0)
        def _():
            for c in (x_copy, k_copy, q_copy):
                c.wait()

        @pl.when(i > 0)
        def _():
            wv_copy(i).wait()

        def rows(m, _):
            at_rows = pl.ds(pl.multiple_of(m * TILE, TILE), TILE)
            proj[at_rows, :] = dot(x[at_rows, :], w[i])
            return 0

        lax.fori_loop(0, ROWS // TILE, rows, 0)

        @pl.when(i == 0)
        def _():
            qk = (proj[...] * 0.5).astype(bf16).astype(f32)
            q32[...] = qk[:, 0:128]
            kt = qk[:, 128:256].T
            kt32[...] = kt
            ktb[...] = kt.astype(bf16)
            lax.fori_loop(0, HEADS, key_features, 0)

        @pl.when(i > 0)
        def _():
            head = 2 * block_of(i)
            v = proj[...].astype(bf16)
            vext[head, :, pl.ds(0, DV)] = v[:, 0:128]
            vext[head + 1, :, pl.ds(0, DV)] = v[:, 128:256]

            def states_of(j, _):
                states[i - 1, j] = state(head + j)
                return 0

            lax.fori_loop(0, PAIR, states_of, 0)

        @pl.when(i == 1)
        def _():
            pl.semaphore_wait(barrier, len(peers))

        @pl.when((i == 1) | (i == 2))
        def _():
            c = i - 1
            send0[c] = states[c].astype(bf16)
            copy0(c).start()

        @pl.when(i >= 3)
        def _():
            c = i - 3
            copy0(c).wait_recv()
            send1[c] = (states[i - 1] + recv0[c].astype(f32)).astype(bf16)
            for k in copies1(c):
                k.start()

        @pl.when(i == 3)
        def _():
            for j in range(8):
                wo_copy(j).start()

        return 0

    lax.fori_loop(0, 5, project, 0)

    c1 = jnp.where(iota((1, FEATS), 1) == 152, 1.0, 0.0)
    c2 = jnp.where((iota((1, FEATS), 1) >= 136) & (iota((1, FEATS), 1) <= 152), 1.0, 0.0)
    is1 = jnp.where(core == 1, 1.0, 0.0).astype(f32)
    before = [jnp.where(lax.rem(pa + 4 - d, 4) < pa, 1.0, 0.0).astype(f32) for d in DISTANCES]

    def local(h, _):
        q = q32[...]
        qm = jnp.where((iota((ROWS, 128), 1) >> 4) == h, q, 0.0).astype(bf16)
        at_row = pl.ds(pl.multiple_of((7 - h) * 16, 16), 128)
        qb = q.astype(bf16)
        f1 = dot(qb, pick1[at_row, :]) + c1
        f2 = dot(qb, pick2[at_row, :]) + c2
        qext[h] = (f1 * f2).astype(bf16)
        below = iota((TILE, TILE), 1) <= iota((TILE, TILE), 0)
        for tb in range(ROWS // TILE):
            span = (tb + 1) * TILE
            r = dot(qm[tb * TILE : span], ktb[:, pl.ds(0, span)])
            wt = (0.5 * r + 1.0) * r + 1.0
            diag = jnp.where(below, wt[:, tb * TILE : span], 0.0).astype(bf16)
            a = dot(diag, vext[h, pl.ds(tb * TILE, TILE), :])
            if tb:
                a = a + dot(wt[:, 0 : tb * TILE].astype(bf16), vext[h, pl.ds(0, tb * TILE), :])
            acc[h, pl.ds(tb * TILE, TILE), :] = a

        @pl.when((h == TURNS[0]) | (h == TURNS[1]))
        def _():
            c = jnp.where(h == TURNS[1], 1, 0)
            for k in copies1(c):
                k.wait_recv()

            def sums_first(j, _):
                got = [recv1[n, c, j].astype(f32) for n in range(3)]
                pre = before[0] * got[0] + before[1] * got[1] + before[2] * got[2]
                every = got[0] + got[1] + got[2]
                send2[0, c, j] = (is1 * pre).astype(bf16)
                send2[1, c, j] = (send1[c, j].astype(f32) + is1 * pre + (1.0 - is1) * every).astype(bf16)
                base[c, j] = pre
                return 0

            lax.fori_loop(0, PAIR, sums_first, 0)
            for k in copies2(c):
                k.start()

        return 0

    lax.fori_loop(0, HEADS, local, 0)

    def set_prefix(h, tile):
        ps[h, :, pl.ds(0, DV)] = tile.astype(bf16)
        row0 = jnp.broadcast_to(tile[153:154], (DV, DV))
        row1 = jnp.broadcast_to(tile[154:155], (DV, DV))
        ps[h, pl.ds(0, 128), pl.ds(DV, DV)] = row0.T.astype(bf16)
        ps[h, pl.ds(128, 32), pl.ds(DV, DV)] = row1.T[0:32].astype(bf16)

    def second(c, _):
        for k in copies2(c):
            k.wait_recv()

        def sums_second(j, _):
            chips = base[c, j] + recv2[0, c, j].astype(f32) + recv2[1, c, j].astype(f32) + recv2[2, c, j].astype(f32)
            send3[c, j] = (chips + (1.0 - is1) * states[2 + c, j]).astype(bf16)
            base[c, j] = chips + is1 * recv0[c, j].astype(f32)
            return 0

        lax.fori_loop(0, PAIR, sums_second, 0)
        copy3(c).start()
        return 0

    lax.fori_loop(0, 2, second, 0)

    def prefixes(i, _):
        c = lax.div(lax.rem(i, 4), 2)
        j = lax.rem(i, 2)
        mine = i < 4

        @pl.when((i == 4) | (i == 6))
        def _():
            copy3(c).wait_recv()

        @pl.when(mine)
        def _():
            states[0, 0] = base[c, j]

        @pl.when(jnp.logical_not(mine))
        def _():
            states[0, 0] = recv3[c, j].astype(f32)

        half = jnp.where(mine, core, 1 - core)
        set_prefix(half * HALF + lax.rem(i, 4), states[0, 0])
        return 0

    lax.fori_loop(0, HEADS, prefixes, 0)

    for j in range(8):
        wo_copy(j).wait()

    def z_copy(j, r):
        to = lax.rem(z + 1 + 2 * lax.rem(j, 2), 4)
        return remote(zs.at[j, r], zr.at[j, r], zss.at[j, r], zrs.at[j, r], at(cx, cy, core, to))

    def rows_phase(r, _):
        at_rows = pl.ds(pl.multiple_of(r * RR, RR), RR)
        for h in range(HEADS):
            a = acc[h, at_rows, :] + dot(qext[h, at_rows, :], ps[h])
            ratio = a[:, 0:DV] / a[:, DV : 2 * DV]
            spread = jnp.mean(ratio * ratio, axis=1, keepdims=True)
            gain = gain_ref[:, pl.ds(h * DV, DV)].astype(f32)
            norm[:, pl.ds(h * DV, DV)] = (ratio * lax.rsqrt(spread + 1e-6) * gain).astype(bf16)

        def sent_parts(j, _):
            zs[j, r] = dot(norm[...], wo[j]).astype(bf16)
            z_copy(j, r).start()
            return 0

        lax.fori_loop(0, 4, sent_parts, 0)

        def kept_parts(j, _):
            part32[j, r] = dot(norm[...], wo[4 + j])
            return 0

        lax.fori_loop(0, 4, kept_parts, 0)
        return 0

    lax.fori_loop(0, RB, rows_phase, 0)

    def combine(r, _):
        for way in range(2):
            z_copy(way, r).wait_recv()
            zs[4 + way, r] = (part32[way, r] + zr[way, r].astype(f32)).astype(bf16)
            z_copy(4 + way, r).start()
        return 0

    lax.fori_loop(0, RB, combine, 0)

    def out_copy(r):
        at_rows = pl.ds(pl.multiple_of(r * RR, RR), RR)
        return pltpu.make_async_copy(obuf.at[r], out_hbm.at[at_rows, :], out_sem.at[r])

    def finish(r, _):
        for j in range(2, 6):
            z_copy(j, r).wait_recv()
        left = part32[2, r] + zr[4, r].astype(f32) + zr[3, r].astype(f32)
        right = part32[3, r] + zr[2, r].astype(f32) + zr[5, r].astype(f32)
        obuf[r, :, pl.ds(0, 512)] = left.astype(bf16)
        obuf[r, :, pl.ds(512, 512)] = right.astype(bf16)
        out_copy(r).start()
        return 0

    lax.fori_loop(0, RB, finish, 0)

    def drain(c, _):
        copy0(c).wait_send()
        copy3(c).wait_send()
        for k in copies1(c) + copies2(c):
            k.wait_send()
        return 0

    lax.fori_loop(0, 2, drain, 0)

    def sent(r, _):
        for j in range(6):
            z_copy(j, r).wait_send()
        out_copy(r).wait()
        return 0

    lax.fori_loop(0, RB, sent, 0)


def per_device(tokens, query_weight, key_weight, value_weight, norm_gain, out_weight):
    dma = pltpu.SemaphoreType.DMA
    hbm = pl.BlockSpec(memory_space=pl.ANY)
    vmem = pl.BlockSpec(memory_space=pltpu.VMEM)
    d = tokens.shape[1]
    tiles = (PAIR, FEATS, DV)
    return pl.pallas_call(
        kernel,
        out_shape=jax.ShapeDtypeStruct((ROWS, 1024), bf16),
        in_specs=[hbm, hbm, hbm, hbm, vmem, hbm],
        out_specs=hbm,
        scratch_shapes=[
            pltpu.VMEM((ROWS, d), bf16),
            pltpu.VMEM((5, d, 256), bf16),
            pltpu.VMEM((8, 1024, 512), bf16),
            pltpu.VMEM((ROWS, 256), f32),
            pltpu.VMEM((ROWS, 128), f32),
            pltpu.VMEM((128, ROWS), f32),
            pltpu.VMEM((128, ROWS), bf16),
            pltpu.VMEM((HEADS, 256, ROWS), bf16),
            pltpu.VMEM((HEADS, ROWS, 2 * DV), bf16),
            pltpu.VMEM((256, FEATS), bf16),
            pltpu.VMEM((256, FEATS), bf16),
            pltpu.VMEM((HEADS, ROWS, FEATS), bf16),
            pltpu.VMEM((HEADS, ROWS, 2 * DV), f32),
            pltpu.VMEM((HEADS, FEATS, 2 * DV), bf16),
            pltpu.VMEM((4,) + tiles, f32),
            pltpu.VMEM((2,) + tiles, bf16),
            pltpu.VMEM((2,) + tiles, bf16),
            pltpu.VMEM((2,) + tiles, bf16),
            pltpu.VMEM((3, 2) + tiles, bf16),
            pltpu.VMEM((2,) + tiles, f32),
            pltpu.VMEM((2, 2) + tiles, bf16),
            pltpu.VMEM((3, 2) + tiles, bf16),
            pltpu.VMEM((2,) + tiles, bf16),
            pltpu.VMEM((2,) + tiles, bf16),
            pltpu.VMEM((RR, 1024), bf16),
            pltpu.VMEM((6, RB, RR, 512), bf16),
            pltpu.VMEM((6, RB, RR, 512), bf16),
            pltpu.VMEM((4, RB, RR, 512), f32),
            pltpu.VMEM((RB, RR, 1024), bf16),
            dma((3,)),
            dma((5,)),
            dma((8,)),
            dma((RB,)),
            dma((2,)), dma((2,)), dma((3, 2)), dma((3, 2)), dma((3, 2)), dma((3, 2)), dma((2,)), dma((2,)),
            dma((6, RB)), dma((6, RB)),
        ],
        compiler_params=pltpu.CompilerParams(
            collective_id=0, has_side_effects=True, vmem_limit_bytes=56 * 1024 * 1024
        ),
    )(tokens, query_weight, key_weight, value_weight, norm_gain.reshape(1, -1), out_weight)


def solution(mesh):
    in_specs = (P("ctx", None), P(None, "tp"), P(None, "tp"), P(None, "tp"), P("tp"), P("tp", None))
    out_specs = P("ctx", "tp")
    return jax.shard_map(
        per_device, mesh=mesh, in_specs=in_specs, out_specs=out_specs, check_vma=False
    )
```

```python
import functools

import jax
import jax.numpy as jnp
from jax import lax
from jax.experimental import pallas as pl
from jax.experimental.pallas import tpu as pltpu
from jax.sharding import PartitionSpec as P

MESH = pl.DeviceIdType.MESH
DV = 128
HEADS = 8
HALF = 4
ROWS = 512
FEATS = 160
TILE = 256
PAIR = 2
TURNS = (3, 6)
DISTANCES = (2, 1, 3)
SLOTS = ((2, 0), (2, 1), (1, 1), (3, 0), (1, 0), (3, 1), (0, 0), (0, 1))
RB = 4
RR = ROWS // RB
f32 = jnp.float32
bf16 = jnp.bfloat16


def iota(shape, axis):
    return lax.broadcasted_iota(jnp.int32, shape, axis)


def dot(a, b):
    return jnp.dot(a, b, preferred_element_type=f32)


def kernel(
    x_hbm, wq_hbm, wk_hbm, wv_hbm, gain_ref, wo_hbm, out_hbm,
    x, w, wo, proj, q32, kt32, ktb, phi, vext, pick1, pick2, qext, acc, ps,
    states, send0, recv0, send1, recv1, base, send2, recv2, send3, recv3,
    norm, gains, zs, zr, part32, obuf,
    in_sem, w_sem, wo_sem, out_sem,
    s0, r0, s1, r1, s2, r2, s3, r3, zss, zrs,
):
    ctx = lax.axis_index("ctx")
    z = lax.axis_index("tp")
    core = lax.rem(ctx, 2)
    cy = lax.rem(lax.div(ctx, 2), 4)
    cx = lax.div(ctx, 8)

    def at(px, py, pc, pz):
        return ((px * 4 + py) * 2 + pc, pz)

    partner = at(cx, cy, 1 - core, z)

    x_copy = pltpu.make_async_copy(x_hbm, x, in_sem.at[0])
    k_copy = pltpu.make_async_copy(wk_hbm, w.at[0, :, pl.ds(128, 128)], in_sem.at[1])
    q_copy = pltpu.make_async_copy(wq_hbm, w.at[0, :, pl.ds(0, 128)], in_sem.at[2])
    for c in (x_copy, k_copy, q_copy):
        c.start()

    def block_of(i):
        return lax.rem(2 * (1 - core) + i - 1, 4)

    def wv_copy(i):
        columns = pl.ds(pl.multiple_of(block_of(i) * 256, 256), 256)
        return pltpu.make_async_copy(wv_hbm.at[:, columns], w.at[i], w_sem.at[i])

    for i in range(1, 5):
        wv_copy(i).start()

    def wo_copy(j):
        chunk, half = SLOTS[j]
        first = lax.rem(z + chunk, 4) * 1024 + half * 512
        columns = pl.ds(pl.multiple_of(first, 512), 512)
        return pltpu.make_async_copy(wo_hbm.at[:, columns], wo.at[j], wo_sem.at[j])

    barrier = pltpu.get_barrier_semaphore()
    peers = [partner]
    for d in (1, 2, 3):
        peers.append(at(lax.rem(cx + d, 4), cy, core, z))
        peers.append(at(cx, lax.rem(cy + d, 4), core, z))
    for d in (1, 3):
        peers.append(at(cx, cy, core, lax.rem(z + d, 4)))
    for p in peers:
        pl.semaphore_signal(barrier, inc=1, device_id=p, device_id_type=MESH)

    def remote(src, dst, ss, rs, dev):
        return pltpu.make_async_remote_copy(
            src_ref=src, dst_ref=dst, send_sem=ss, recv_sem=rs, device_id=dev, device_id_type=MESH
        )

    row = iota((256, FEATS), 0) - 112
    col = iota((256, FEATS), 1)
    low = col & 15
    first = jnp.where(col < 136, low, col - 136)
    second = (low + (col >> 4)) & 15
    pick1[...] = jnp.where((row == first) & (col < 152), 1.0, 0.0).astype(bf16)
    pick2[...] = jnp.where((row == second) & (col < 136), 1.0, 0.0).astype(bf16)
    phi[:, pl.ds(FEATS, 256 - FEATS), :] = jnp.zeros((HEADS, 256 - FEATS, ROWS), bf16)
    for h in range(HEADS):
        at_head = pl.ds(h * DV, DV)
        gains[0:1, at_head] = gain_ref[at_head].astype(f32).reshape(1, DV)
    vext[:, :, pl.ds(DV, DV)] = jnp.ones((HEADS, ROWS, DV), bf16)

    ones16 = jnp.ones((16, ROWS), bf16)

    def key_features(h, _):
        k = kt32[pl.ds(pl.multiple_of(h * 16, 16), 16), :]
        parts = [k * k * 0.5]
        for o in range(1, 8):
            parts.append(k * pltpu.roll(k, 16 - o, 0))
        parts.append(k[0:8] * k[8:16])
        parts.append(k)
        parts.append(jnp.where(iota((8, ROWS), 0) == 0, 1.0, 0.0))
        phi[h, pl.ds(0, FEATS), :] = jnp.concatenate(parts, axis=0).astype(bf16)
        return 0

    def state(h):
        p = phi[h, pl.ds(0, FEATS), :]
        st = dot(p, vext[h, :, pl.ds(0, DV)])
        nt = (((1,), (1,)), ((), ()))
        sums = lax.dot_general(ones16, phi[h], nt, preferred_element_type=f32)
        i8 = iota((8, DV), 0)
        last = st[152:160] + jnp.where(i8 == 1, sums[0:8, 0:DV], 0.0) + jnp.where(i8 == 2, sums[0:8, DV:], 0.0)
        return jnp.concatenate([st[0:152], last], axis=0)

    pa = jnp.where(core == 0, cy, cx)
    pb = jnp.where(core == 0, cx, cy)

    def on_axes(a, b):
        return at(jnp.where(core == 0, b, a), jnp.where(core == 0, a, b), core, z)

    def copy0(c):
        return remote(send0.at[c], recv0.at[c], s0.at[c], r0.at[c], partner)

    def needed1(sender, receiver):
        return (core == 0) | (sender < receiver)

    def needed2(sender, receiver):
        return (core == 1) | (sender < receiver)

    def copies1(c):
        out = []
        for n, d in enumerate(DISTANCES):
            to, source = lax.rem(pa + d, 4), lax.rem(pa + 4 - d, 4)
            copy = remote(send1.at[c], recv1.at[n, c], s1.at[n, c], r1.at[n, c], on_axes(to, pb))
            out.append((copy, needed1(pa, to), needed1(source, pa)))
        return out

    def copies2(c):
        out = []
        for n, d in enumerate(DISTANCES):
            to, source = lax.rem(pb + d, 4), lax.rem(pb + 4 - d, 4)
            kind = jnp.where(to > pb, 1, 0)
            copy = remote(send2.at[kind, c], recv2.at[n, c], s2.at[n, c], r2.at[n, c], on_axes(pa, to))
            out.append((copy, needed2(pb, to), needed2(source, pb)))
        return out

    def start(copies):
        for copy, sends, _ in copies:
            pl.when(sends)(copy.start)

    def wait_recv(copies):
        for copy, _, receives in copies:
            pl.when(receives)(copy.wait_recv)

    def wait_send(copies):
        for copy, sends, _ in copies:
            pl.when(sends)(copy.wait_send)

    for buffer, copies in ((recv1, copies1(0)), (recv2, copies2(0))):
        for n, (_, _, receives) in enumerate(copies):

            @pl.when(jnp.logical_not(receives))
            def _():
                buffer[n] = jnp.zeros((2, PAIR, FEATS, DV), bf16)

    def copy3(c):
        return remote(send3.at[c], recv3.at[c], s3.at[c], r3.at[c], partner)

    def project(i, _):
        @pl.when(i == 0)
        def _():
            for c in (x_copy, k_copy, q_copy):
                c.wait()

        @pl.when(i > 0)
        def _():
            wv_copy(i).wait()

        def rows(m, _):
            at_rows = pl.ds(pl.multiple_of(m * TILE, TILE), TILE)
            proj[at_rows, :] = dot(x[at_rows, :], w[i])
            return 0

        lax.fori_loop(0, ROWS // TILE, rows, 0)

        @pl.when(i == 0)
        def _():
            qk = (proj[...] * 0.5).astype(bf16).astype(f32)
            q32[...] = qk[:, 0:128]
            kt = qk[:, 128:256].T
            kt32[...] = kt
            ktb[...] = kt.astype(bf16)
            lax.fori_loop(0, HEADS, key_features, 0)

        @pl.when(i > 0)
        def _():
            head = 2 * block_of(i)
            v = proj[...].astype(bf16)
            vext[head, :, pl.ds(0, DV)] = v[:, 0:128]
            vext[head + 1, :, pl.ds(0, DV)] = v[:, 128:256]

            def states_of(j, _):
                states[i - 1, j] = state(head + j)
                return 0

            lax.fori_loop(0, PAIR, states_of, 0)

        @pl.when(i == 1)
        def _():
            pl.semaphore_wait(barrier, len(peers))

        @pl.when((i == 1) | (i == 2))
        def _():
            c = i - 1
            send0[c] = states[c].astype(bf16)
            copy0(c).start()

        @pl.when(i >= 3)
        def _():
            c = i - 3
            copy0(c).wait_recv()
            send1[c] = (states[i - 1] + recv0[c].astype(f32)).astype(bf16)
            start(copies1(c))

        @pl.when(i == 3)
        def _():
            for j in range(8):
                wo_copy(j).start()

        return 0

    lax.fori_loop(0, 5, project, 0)

    c1 = jnp.where(iota((1, FEATS), 1) == 152, 1.0, 0.0)
    c2 = jnp.where((iota((1, FEATS), 1) >= 136) & (iota((1, FEATS), 1) <= 152), 1.0, 0.0)
    is1 = jnp.where(core == 1, 1.0, 0.0).astype(f32)
    before = [jnp.where(lax.rem(pa + 4 - d, 4) < pa, 1.0, 0.0).astype(f32) for d in DISTANCES]

    def local(h, _):
        q = q32[...]
        qm = jnp.where((iota((ROWS, 128), 1) >> 4) == h, q, 0.0).astype(bf16)
        at_row = pl.ds(pl.multiple_of((7 - h) * 16, 16), 128)
        qb = q.astype(bf16)
        f1 = dot(qb, pick1[at_row, :]) + c1
        f2 = dot(qb, pick2[at_row, :]) + c2
        qext[h] = (f1 * f2).astype(bf16)
        below = iota((TILE, TILE), 1) <= iota((TILE, TILE), 0)
        for tb in range(ROWS // TILE):
            span = (tb + 1) * TILE
            r = dot(qm[tb * TILE : span], ktb[:, pl.ds(0, span)])
            wt = (0.5 * r + 1.0) * r + 1.0
            diag = jnp.where(below, wt[:, tb * TILE : span], 0.0).astype(bf16)
            a = dot(diag, vext[h, pl.ds(tb * TILE, TILE), :])
            if tb:
                a = a + dot(wt[:, 0 : tb * TILE].astype(bf16), vext[h, pl.ds(0, tb * TILE), :])
            acc[h, pl.ds(tb * TILE, TILE), :] = a

        @pl.when((h == TURNS[0]) | (h == TURNS[1]))
        def _():
            c = jnp.where(h == TURNS[1], 1, 0)
            wait_recv(copies1(c))

            def sums_first(j, _):
                got = [recv1[n, c, j].astype(f32) for n in range(3)]
                pre = before[0] * got[0] + before[1] * got[1] + before[2] * got[2]
                every = got[0] + got[1] + got[2]
                send2[0, c, j] = (is1 * pre).astype(bf16)
                send2[1, c, j] = (send1[c, j].astype(f32) + is1 * pre + (1.0 - is1) * every).astype(bf16)
                base[c, j] = pre
                return 0

            lax.fori_loop(0, PAIR, sums_first, 0)
            start(copies2(c))

        return 0

    lax.fori_loop(0, HEADS, local, 0)

    def set_prefix(h, tile):
        ps[h, :, pl.ds(0, DV)] = tile.astype(bf16)
        row0 = jnp.broadcast_to(tile[153:154], (DV, DV))
        row1 = jnp.broadcast_to(tile[154:155], (DV, DV))
        ps[h, pl.ds(0, 128), pl.ds(DV, DV)] = row0.T.astype(bf16)
        ps[h, pl.ds(128, 32), pl.ds(DV, DV)] = row1.T[0:32].astype(bf16)

    def normalize(h, at_rows):
        at_head = pl.ds(pl.multiple_of(h * DV, DV), DV)
        a = acc[h, at_rows, :] + dot(qext[h, at_rows, :], ps[h])
        ratio = a[:, 0:DV] / a[:, DV : 2 * DV]
        spread = jnp.mean(ratio * ratio, axis=1, keepdims=True)
        norm[at_rows, at_head] = (ratio * lax.rsqrt(spread + 1e-6) * gains[0:1, at_head]).astype(bf16)

    def second(c, _):
        wait_recv(copies2(c))

        def sums_second(j, _):
            chips = base[c, j] + recv2[0, c, j].astype(f32) + recv2[1, c, j].astype(f32) + recv2[2, c, j].astype(f32)
            send3[c, j] = (chips + (1.0 - is1) * states[2 + c, j]).astype(bf16)
            base[c, j] = chips + is1 * recv0[c, j].astype(f32)
            return 0

        lax.fori_loop(0, PAIR, sums_second, 0)
        copy3(c).start()

        def own_prefix(j, _):
            h = core * HALF + c * PAIR + j
            set_prefix(h, base[c, j])
            normalize(h, pl.ds(0, ROWS))
            return 0

        lax.fori_loop(0, PAIR, own_prefix, 0)
        return 0

    lax.fori_loop(0, 2, second, 0)

    def prefixes(i, _):
        c, j = lax.div(i, 2), lax.rem(i, 2)

        @pl.when(j == 0)
        def _():
            copy3(c).wait_recv()

        set_prefix((1 - core) * HALF + i, recv3[c, j].astype(f32))
        return 0

    lax.fori_loop(0, HALF, prefixes, 0)

    for j in range(8):
        wo_copy(j).wait()

    def z_copy(j, r):
        to = lax.rem(z + 1 + 2 * lax.rem(j, 2), 4)
        return remote(zs.at[j, r], zr.at[j, r], zss.at[j, r], zrs.at[j, r], at(cx, cy, core, to))

    def rows_phase(r, _):
        at_rows = pl.ds(pl.multiple_of(r * RR, RR), RR)
        for i in range(HALF):
            normalize((1 - core) * HALF + i, at_rows)

        def sent_parts(j, _):
            zs[j, r] = dot(norm[at_rows, :], wo[j]).astype(bf16)
            z_copy(j, r).start()
            return 0

        lax.fori_loop(0, 4, sent_parts, 0)

        def kept_parts(j, _):
            part32[j, r] = dot(norm[at_rows, :], wo[4 + j])
            return 0

        lax.fori_loop(0, 4, kept_parts, 0)
        return 0

    lax.fori_loop(0, RB, rows_phase, 0)

    def combine(r, _):
        for way in range(2):
            z_copy(way, r).wait_recv()
            zs[4 + way, r] = (part32[way, r] + zr[way, r].astype(f32)).astype(bf16)
            z_copy(4 + way, r).start()
        return 0

    lax.fori_loop(0, RB, combine, 0)

    def out_copy(r):
        at_rows = pl.ds(pl.multiple_of(r * RR, RR), RR)
        return pltpu.make_async_copy(obuf.at[r], out_hbm.at[at_rows, :], out_sem.at[r])

    def finish(r, _):
        for j in range(2, 6):
            z_copy(j, r).wait_recv()
        left = part32[2, r] + zr[4, r].astype(f32) + zr[3, r].astype(f32)
        right = part32[3, r] + zr[2, r].astype(f32) + zr[5, r].astype(f32)
        obuf[r, :, pl.ds(0, 512)] = left.astype(bf16)
        obuf[r, :, pl.ds(512, 512)] = right.astype(bf16)
        out_copy(r).start()
        return 0

    lax.fori_loop(0, RB, finish, 0)

    def drain(c, _):
        copy0(c).wait_send()
        copy3(c).wait_send()
        wait_send(copies1(c))
        wait_send(copies2(c))
        return 0

    lax.fori_loop(0, 2, drain, 0)

    def sent(r, _):
        for j in range(6):
            z_copy(j, r).wait_send()
        out_copy(r).wait()
        return 0

    lax.fori_loop(0, RB, sent, 0)


def per_device(tokens, query_weight, key_weight, value_weight, norm_gain, out_weight):
    dma = pltpu.SemaphoreType.DMA
    hbm = pl.BlockSpec(memory_space=pltpu.HBM)
    vmem = pl.BlockSpec(memory_space=pltpu.VMEM)
    d = tokens.shape[1]
    tiles = (PAIR, FEATS, DV)
    return pl.pallas_call(
        kernel,
        out_shape=jax.ShapeDtypeStruct((ROWS, 1024), bf16),
        in_specs=[hbm, hbm, hbm, hbm, vmem, hbm],
        out_specs=pl.BlockSpec(memory_space=pl.ANY),
        scratch_shapes=[
            pltpu.VMEM((ROWS, d), bf16),
            pltpu.VMEM((5, d, 256), bf16),
            pltpu.VMEM((8, 1024, 512), bf16),
            pltpu.VMEM((ROWS, 256), f32),
            pltpu.VMEM((ROWS, 128), f32),
            pltpu.VMEM((128, ROWS), f32),
            pltpu.VMEM((128, ROWS), bf16),
            pltpu.VMEM((HEADS, 256, ROWS), bf16),
            pltpu.VMEM((HEADS, ROWS, 2 * DV), bf16),
            pltpu.VMEM((256, FEATS), bf16),
            pltpu.VMEM((256, FEATS), bf16),
            pltpu.VMEM((HEADS, ROWS, FEATS), bf16),
            pltpu.VMEM((HEADS, ROWS, 2 * DV), f32),
            pltpu.VMEM((HEADS, FEATS, 2 * DV), bf16),
            pltpu.VMEM((4,) + tiles, f32),
            pltpu.VMEM((2,) + tiles, bf16),
            pltpu.VMEM((2,) + tiles, bf16),
            pltpu.VMEM((2,) + tiles, bf16),
            pltpu.VMEM((3, 2) + tiles, bf16),
            pltpu.VMEM((2,) + tiles, f32),
            pltpu.VMEM((2, 2) + tiles, bf16),
            pltpu.VMEM((3, 2) + tiles, bf16),
            pltpu.VMEM((2,) + tiles, bf16),
            pltpu.VMEM((2,) + tiles, bf16),
            pltpu.VMEM((ROWS, 1024), bf16),
            pltpu.VMEM((8, 1024), f32),
            pltpu.VMEM((6, RB, RR, 512), bf16),
            pltpu.VMEM((6, RB, RR, 512), bf16),
            pltpu.VMEM((4, RB, RR, 512), f32),
            pltpu.VMEM((RB, RR, 1024), bf16),
            dma((3,)),
            dma((5,)),
            dma((8,)),
            dma((RB,)),
            dma((2,)), dma((2,)), dma((3, 2)), dma((3, 2)), dma((3, 2)), dma((3, 2)), dma((2,)), dma((2,)),
            dma((6, RB)), dma((6, RB)),
        ],
        compiler_params=pltpu.CompilerParams(
            collective_id=0, has_side_effects=True, vmem_limit_bytes=52 * 1024 * 1024
        ),
    )(tokens, query_weight, key_weight, value_weight, norm_gain, out_weight)


def solution(mesh):
    in_specs = (P("ctx", None), P(None, "tp"), P(None, "tp"), P(None, "tp"), P("tp"), P("tp", None))
    out_specs = P("ctx", "tp")
    return jax.shard_map(
        per_device, mesh=mesh, in_specs=in_specs, out_specs=out_specs, check_vma=False
    )
```

```python
import functools

import jax
import jax.numpy as jnp
from jax import lax
from jax.experimental import pallas as pl
from jax.experimental.pallas import tpu as pltpu
from jax.sharding import PartitionSpec as P

MESH = pl.DeviceIdType.MESH
DV = 128
HEADS = 8
HALF = 4
ROWS = 512
FEATS = 160
TILE = 256
PAIR = 2
TURNS = (3, 6)
DISTANCES = (2, 1, 3)
SLOTS = ((2, 0), (2, 1), (1, 1), (3, 0), (1, 0), (3, 1), (0, 0), (0, 1))
RB = 4
RR = ROWS // RB
f32 = jnp.float32
bf16 = jnp.bfloat16


def iota(shape, axis):
    return lax.broadcasted_iota(jnp.int32, shape, axis)


def dot(a, b):
    return jnp.dot(a, b, preferred_element_type=f32)


def kernel(
    x_hbm, wq_hbm, wk_hbm, wv_hbm, gain_ref, wo_hbm, out_hbm,
    x, w, wo, proj, q32, kt32, ktb, phi, vext, pick1, pick2, qext, acc, ps,
    states, send0, recv0, send1, recv1, base, send2, recv2, send3, recv3,
    norm, gains, zs, zr, part32, obuf,
    in_sem, w_sem, wo_sem, out_sem,
    s0, r0, s1, r1, s2, r2, s3, r3, zss, zrs,
):
    ctx = lax.axis_index("ctx")
    z = lax.axis_index("tp")
    core = lax.rem(ctx, 2)
    cy = lax.rem(lax.div(ctx, 2), 4)
    cx = lax.div(ctx, 8)

    def at(px, py, pc, pz):
        return ((px * 4 + py) * 2 + pc, pz)

    partner = at(cx, cy, 1 - core, z)

    x_copy = pltpu.make_async_copy(x_hbm, x, in_sem.at[0])
    k_copy = pltpu.make_async_copy(wk_hbm, w.at[0, :, pl.ds(128, 128)], in_sem.at[1])
    q_copy = pltpu.make_async_copy(wq_hbm, w.at[0, :, pl.ds(0, 128)], in_sem.at[2])
    for c in (x_copy, k_copy, q_copy):
        c.start()

    def block_of(i):
        return lax.rem(2 * (1 - core) + i - 1, 4)

    def wv_copy(i):
        columns = pl.ds(pl.multiple_of(block_of(i) * 256, 256), 256)
        return pltpu.make_async_copy(wv_hbm.at[:, columns], w.at[i], w_sem.at[i])

    for i in range(1, 5):
        wv_copy(i).start()

    def wo_copy(j):
        chunk, half = SLOTS[j]
        first = lax.rem(z + chunk, 4) * 1024 + half * 512
        columns = pl.ds(pl.multiple_of(first, 512), 512)
        return pltpu.make_async_copy(wo_hbm.at[:, columns], wo.at[j], wo_sem.at[j])

    barrier = pltpu.get_barrier_semaphore()
    peers = [partner]
    for d in (1, 2, 3):
        peers.append(at(lax.rem(cx + d, 4), cy, core, z))
        peers.append(at(cx, lax.rem(cy + d, 4), core, z))
    for d in (1, 3):
        peers.append(at(cx, cy, core, lax.rem(z + d, 4)))
    for p in peers:
        pl.semaphore_signal(barrier, inc=1, device_id=p, device_id_type=MESH)

    def remote(src, dst, ss, rs, dev):
        return pltpu.make_async_remote_copy(
            src_ref=src, dst_ref=dst, send_sem=ss, recv_sem=rs, device_id=dev, device_id_type=MESH
        )

    row = iota((256, FEATS), 0) - 112
    col = iota((256, FEATS), 1)
    low = col & 15
    first = jnp.where(col < 136, low, col - 136)
    second = (low + (col >> 4)) & 15
    pick1[...] = jnp.where((row == first) & (col < 152), 1.0, 0.0).astype(bf16)
    pick2[...] = jnp.where((row == second) & (col < 136), 1.0, 0.0).astype(bf16)
    phi[:, pl.ds(FEATS, 256 - FEATS), :] = jnp.zeros((HEADS, 256 - FEATS, ROWS), bf16)
    for h in range(HEADS):
        at_head = pl.ds(h * DV, DV)
        gains[0:1, at_head] = gain_ref[at_head].astype(f32).reshape(1, DV)
    vext[:, :, pl.ds(DV, DV)] = jnp.ones((HEADS, ROWS, DV), bf16)

    ones16 = jnp.ones((16, ROWS), bf16)

    def key_features(h, _):
        k = kt32[pl.ds(pl.multiple_of(h * 16, 16), 16), :]
        parts = [k * k * 0.5]
        for o in range(1, 8):
            parts.append(k * pltpu.roll(k, 16 - o, 0))
        parts.append(k[0:8] * k[8:16])
        parts.append(k)
        parts.append(jnp.where(iota((8, ROWS), 0) == 0, 1.0, 0.0))
        phi[h, pl.ds(0, FEATS), :] = jnp.concatenate(parts, axis=0).astype(bf16)
        return 0

    def state(h):
        p = phi[h, pl.ds(0, FEATS), :]
        st = dot(p, vext[h, :, pl.ds(0, DV)])
        nt = (((1,), (1,)), ((), ()))
        sums = lax.dot_general(ones16, phi[h], nt, preferred_element_type=f32)
        i8 = iota((8, DV), 0)
        last = st[152:160] + jnp.where(i8 == 1, sums[0:8, 0:DV], 0.0) + jnp.where(i8 == 2, sums[0:8, DV:], 0.0)
        return jnp.concatenate([st[0:152], last], axis=0)

    pa = jnp.where(core == 0, cy, cx)
    pb = jnp.where(core == 0, cx, cy)

    def on_axes(a, b):
        return at(jnp.where(core == 0, b, a), jnp.where(core == 0, a, b), core, z)

    def copy0(c):
        return remote(send0.at[c], recv0.at[c], s0.at[c], r0.at[c], partner)

    def needed1(sender, receiver):
        return (core == 0) | (sender < receiver)

    def needed2(sender, receiver):
        return (core == 1) | (sender < receiver)

    def copies1(c):
        out = []
        for n, d in enumerate(DISTANCES):
            to, source = lax.rem(pa + d, 4), lax.rem(pa + 4 - d, 4)
            copy = remote(send1.at[c], recv1.at[n, c], s1.at[n, c], r1.at[n, c], on_axes(to, pb))
            out.append((copy, needed1(pa, to), needed1(source, pa)))
        return out

    def copies2(c):
        out = []
        for n, d in enumerate(DISTANCES):
            to, source = lax.rem(pb + d, 4), lax.rem(pb + 4 - d, 4)
            kind = jnp.where(to > pb, 1, 0)
            copy = remote(send2.at[kind, c], recv2.at[n, c], s2.at[n, c], r2.at[n, c], on_axes(pa, to))
            out.append((copy, needed2(pb, to), needed2(source, pb)))
        return out

    def start(copies):
        for copy, sends, _ in copies:
            pl.when(sends)(copy.start)

    def wait_recv(copies):
        for copy, _, receives in copies:
            pl.when(receives)(copy.wait_recv)

    def wait_send(copies):
        for copy, sends, _ in copies:
            pl.when(sends)(copy.wait_send)

    for buffer, copies in ((recv1, copies1(0)), (recv2, copies2(0))):
        for n, (_, _, receives) in enumerate(copies):

            @pl.when(jnp.logical_not(receives))
            def _():
                buffer[n] = jnp.zeros((2, PAIR, FEATS, DV), bf16)

    def copy3(c):
        return remote(send3.at[c], recv3.at[c], s3.at[c], r3.at[c], partner)

    def project(i, _):
        @pl.when(i == 0)
        def _():
            for c in (x_copy, k_copy, q_copy):
                c.wait()

        @pl.when(i > 0)
        def _():
            wv_copy(i).wait()

        def rows(m, _):
            at_rows = pl.ds(pl.multiple_of(m * TILE, TILE), TILE)
            proj[at_rows, :] = dot(x[at_rows, :], w[i])
            return 0

        lax.fori_loop(0, ROWS // TILE, rows, 0, unroll=True)

        @pl.when(i == 0)
        def _():
            qk = (proj[...] * 0.5).astype(bf16).astype(f32)
            q32[...] = qk[:, 0:128]
            kt = qk[:, 128:256].T
            kt32[...] = kt
            ktb[...] = kt.astype(bf16)
            lax.fori_loop(0, HEADS, key_features, 0)

        @pl.when(i > 0)
        def _():
            head = 2 * block_of(i)
            v = proj[...].astype(bf16)
            vext[head, :, pl.ds(0, DV)] = v[:, 0:128]
            vext[head + 1, :, pl.ds(0, DV)] = v[:, 128:256]

            def states_of(j, _):
                states[i - 1, j] = state(head + j)
                return 0

            lax.fori_loop(0, PAIR, states_of, 0, unroll=True)

        @pl.when(i == 1)
        def _():
            pl.semaphore_wait(barrier, len(peers))

        @pl.when((i == 1) | (i == 2))
        def _():
            c = i - 1
            send0[c] = states[c].astype(bf16)
            copy0(c).start()

        @pl.when(i >= 3)
        def _():
            c = i - 3
            copy0(c).wait_recv()
            send1[c] = (states[i - 1] + recv0[c].astype(f32)).astype(bf16)
            start(copies1(c))

        @pl.when(i == 3)
        def _():
            for j in range(8):
                wo_copy(j).start()

        return 0

    lax.fori_loop(0, 5, project, 0)

    c1 = jnp.where(iota((1, FEATS), 1) == 152, 1.0, 0.0)
    c2 = jnp.where((iota((1, FEATS), 1) >= 136) & (iota((1, FEATS), 1) <= 152), 1.0, 0.0)
    is1 = jnp.where(core == 1, 1.0, 0.0).astype(f32)
    before = [jnp.where(lax.rem(pa + 4 - d, 4) < pa, 1.0, 0.0).astype(f32) for d in DISTANCES]

    def local(h, _):
        q = q32[...]
        qm = jnp.where((iota((ROWS, 128), 1) >> 4) == h, q, 0.0).astype(bf16)
        at_row = pl.ds(pl.multiple_of((7 - h) * 16, 16), 128)
        qb = q.astype(bf16)
        f1 = dot(qb, pick1[at_row, :]) + c1
        f2 = dot(qb, pick2[at_row, :]) + c2
        qext[h] = (f1 * f2).astype(bf16)
        below = iota((TILE, TILE), 1) <= iota((TILE, TILE), 0)
        for tb in range(ROWS // TILE):
            span = (tb + 1) * TILE
            r = dot(qm[tb * TILE : span], ktb[:, pl.ds(0, span)])
            wt = (0.5 * r + 1.0) * r + 1.0
            diag = jnp.where(below, wt[:, tb * TILE : span], 0.0).astype(bf16)
            a = dot(diag, vext[h, pl.ds(tb * TILE, TILE), :])
            if tb:
                a = a + dot(wt[:, 0 : tb * TILE].astype(bf16), vext[h, pl.ds(0, tb * TILE), :])
            acc[h, pl.ds(tb * TILE, TILE), :] = a

        @pl.when((h == TURNS[0]) | (h == TURNS[1]))
        def _():
            c = jnp.where(h == TURNS[1], 1, 0)
            wait_recv(copies1(c))

            def sums_first(j, _):
                got = [recv1[n, c, j].astype(f32) for n in range(3)]
                pre = before[0] * got[0] + before[1] * got[1] + before[2] * got[2]
                every = got[0] + got[1] + got[2]
                send2[0, c, j] = (is1 * pre).astype(bf16)
                send2[1, c, j] = (send1[c, j].astype(f32) + is1 * pre + (1.0 - is1) * every).astype(bf16)
                base[c, j] = pre
                return 0

            lax.fori_loop(0, PAIR, sums_first, 0)
            start(copies2(c))

        return 0

    lax.fori_loop(0, HEADS, local, 0)

    def set_prefix(h, tile):
        ps[h, :, pl.ds(0, DV)] = tile.astype(bf16)
        row0 = jnp.broadcast_to(tile[153:154], (DV, DV))
        row1 = jnp.broadcast_to(tile[154:155], (DV, DV))
        ps[h, pl.ds(0, 128), pl.ds(DV, DV)] = row0.T.astype(bf16)
        ps[h, pl.ds(128, 32), pl.ds(DV, DV)] = row1.T[0:32].astype(bf16)

    def normalize(h, at_rows):
        at_head = pl.ds(pl.multiple_of(h * DV, DV), DV)
        a = acc[h, at_rows, :] + dot(qext[h, at_rows, :], ps[h])
        ratio = a[:, 0:DV] / a[:, DV : 2 * DV]
        spread = jnp.mean(ratio * ratio, axis=1, keepdims=True)
        norm[at_rows, at_head] = (ratio * lax.rsqrt(spread + 1e-6) * gains[0:1, at_head]).astype(bf16)

    def second(c, _):
        wait_recv(copies2(c))

        def sums_second(j, _):
            chips = base[c, j] + recv2[0, c, j].astype(f32) + recv2[1, c, j].astype(f32) + recv2[2, c, j].astype(f32)
            send3[c, j] = (chips + (1.0 - is1) * states[2 + c, j]).astype(bf16)
            base[c, j] = chips + is1 * recv0[c, j].astype(f32)
            return 0

        lax.fori_loop(0, PAIR, sums_second, 0)
        copy3(c).start()

        def own_prefix(j, _):
            h = core * HALF + c * PAIR + j
            set_prefix(h, base[c, j])
            normalize(h, pl.ds(0, ROWS))
            return 0

        lax.fori_loop(0, PAIR, own_prefix, 0)
        return 0

    lax.fori_loop(0, 2, second, 0)

    def prefixes(i, _):
        c, j = lax.div(i, 2), lax.rem(i, 2)

        @pl.when(j == 0)
        def _():
            copy3(c).wait_recv()

        set_prefix((1 - core) * HALF + i, recv3[c, j].astype(f32))
        return 0

    lax.fori_loop(0, HALF, prefixes, 0)

    for j in range(8):
        wo_copy(j).wait()

    def z_copy(j, r):
        to = lax.rem(z + 1 + 2 * lax.rem(j, 2), 4)
        return remote(zs.at[j, r], zr.at[j, r], zss.at[j, r], zrs.at[j, r], at(cx, cy, core, to))

    def rows_phase(r, _):
        at_rows = pl.ds(pl.multiple_of(r * RR, RR), RR)
        for i in range(HALF):
            normalize((1 - core) * HALF + i, at_rows)

        def sent_parts(j, _):
            zs[j, r] = dot(norm[at_rows, :], wo[j]).astype(bf16)
            z_copy(j, r).start()
            return 0

        lax.fori_loop(0, 4, sent_parts, 0, unroll=True)

        def kept_parts(j, _):
            part32[j, r] = dot(norm[at_rows, :], wo[4 + j])
            return 0

        lax.fori_loop(0, 4, kept_parts, 0)
        return 0

    lax.fori_loop(0, RB, rows_phase, 0)

    def combine(r, _):
        for way in range(2):
            z_copy(way, r).wait_recv()
            zs[4 + way, r] = (part32[way, r] + zr[way, r].astype(f32)).astype(bf16)
            z_copy(4 + way, r).start()
        return 0

    lax.fori_loop(0, RB, combine, 0)

    def out_copy(r):
        at_rows = pl.ds(pl.multiple_of(r * RR, RR), RR)
        return pltpu.make_async_copy(obuf.at[r], out_hbm.at[at_rows, :], out_sem.at[r])

    def finish(r, _):
        for j in range(2, 6):
            z_copy(j, r).wait_recv()
        left = part32[2, r] + zr[4, r].astype(f32) + zr[3, r].astype(f32)
        right = part32[3, r] + zr[2, r].astype(f32) + zr[5, r].astype(f32)
        obuf[r, :, pl.ds(0, 512)] = left.astype(bf16)
        obuf[r, :, pl.ds(512, 512)] = right.astype(bf16)
        out_copy(r).start()
        return 0

    lax.fori_loop(0, RB, finish, 0)

    def drain(c, _):
        copy0(c).wait_send()
        copy3(c).wait_send()
        wait_send(copies1(c))
        wait_send(copies2(c))
        return 0

    lax.fori_loop(0, 2, drain, 0)

    def sent(r, _):
        for j in range(6):
            z_copy(j, r).wait_send()
        out_copy(r).wait()
        return 0

    lax.fori_loop(0, RB, sent, 0)


def per_device(tokens, query_weight, key_weight, value_weight, norm_gain, out_weight):
    dma = pltpu.SemaphoreType.DMA
    hbm = pl.BlockSpec(memory_space=pltpu.HBM)
    vmem = pl.BlockSpec(memory_space=pltpu.VMEM)
    d = tokens.shape[1]
    tiles = (PAIR, FEATS, DV)
    return pl.pallas_call(
        kernel,
        out_shape=jax.ShapeDtypeStruct((ROWS, 1024), bf16),
        in_specs=[hbm, hbm, hbm, hbm, vmem, hbm],
        out_specs=pl.BlockSpec(memory_space=pl.ANY),
        scratch_shapes=[
            pltpu.VMEM((ROWS, d), bf16),
            pltpu.VMEM((5, d, 256), bf16),
            pltpu.VMEM((8, 1024, 512), bf16),
            pltpu.VMEM((ROWS, 256), f32),
            pltpu.VMEM((ROWS, 128), f32),
            pltpu.VMEM((128, ROWS), f32),
            pltpu.VMEM((128, ROWS), bf16),
            pltpu.VMEM((HEADS, 256, ROWS), bf16),
            pltpu.VMEM((HEADS, ROWS, 2 * DV), bf16),
            pltpu.VMEM((256, FEATS), bf16),
            pltpu.VMEM((256, FEATS), bf16),
            pltpu.VMEM((HEADS, ROWS, FEATS), bf16),
            pltpu.VMEM((HEADS, ROWS, 2 * DV), f32),
            pltpu.VMEM((HEADS, FEATS, 2 * DV), bf16),
            pltpu.VMEM((4,) + tiles, f32),
            pltpu.VMEM((2,) + tiles, bf16),
            pltpu.VMEM((2,) + tiles, bf16),
            pltpu.VMEM((2,) + tiles, bf16),
            pltpu.VMEM((3, 2) + tiles, bf16),
            pltpu.VMEM((2,) + tiles, f32),
            pltpu.VMEM((2, 2) + tiles, bf16),
            pltpu.VMEM((3, 2) + tiles, bf16),
            pltpu.VMEM((2,) + tiles, bf16),
            pltpu.VMEM((2,) + tiles, bf16),
            pltpu.VMEM((ROWS, 1024), bf16),
            pltpu.VMEM((8, 1024), f32),
            pltpu.VMEM((6, RB, RR, 512), bf16),
            pltpu.VMEM((6, RB, RR, 512), bf16),
            pltpu.VMEM((4, RB, RR, 512), f32),
            pltpu.VMEM((RB, RR, 1024), bf16),
            dma((3,)),
            dma((5,)),
            dma((8,)),
            dma((RB,)),
            dma((2,)), dma((2,)), dma((3, 2)), dma((3, 2)), dma((3, 2)), dma((3, 2)), dma((2,)), dma((2,)),
            dma((6, RB)), dma((6, RB)),
        ],
        compiler_params=pltpu.CompilerParams(
            collective_id=0, has_side_effects=True, vmem_limit_bytes=52 * 1024 * 1024
        ),
    )(tokens, query_weight, key_weight, value_weight, norm_gain, out_weight)


def solution(mesh):
    in_specs = (P("ctx", None), P(None, "tp"), P(None, "tp"), P(None, "tp"), P("tp"), P("tp", None))
    out_specs = P("ctx", "tp")
    return jax.shard_map(
        per_device, mesh=mesh, in_specs=in_specs, out_specs=out_specs, check_vma=False
    )
```
